32 devices in a mesh: tile: 8 (over y, x, core), mp: 4 (over z).
Axes of the slice: x: 2, y: 2, z: 4, core: 2. Of those that a mesh axis runs over, the one named last changes fastest.
Arguments:
- tokens: bfloat16 [64, 256, 1024], P('tile', 'mp'), may hold values from -6 to 6
- ln_gain_one: float32 [1024], replicated, may hold values from 0.5 to 1.5
- ln_gain_two: float32 [1024], replicated, may hold values from 0.5 to 1.5
- qkv_weight: bfloat16 [3, 1024, 1024], P(None, None, 'mp'), may hold values from -2 to 2
- out_weight: bfloat16 [1024, 1024], P('mp'), may hold values from -0.1875 to 0.1875
- in_weight: bfloat16 [4096, 1024], P('mp'), may hold values from -0.1875 to 0.1875
- mlp_out_weight: bfloat16 [4096, 1024], P('mp'), may hold values from -0.09375 to 0.09375
- proj_weight: bfloat16 [1024, 256], replicated, may hold values from -0.1875 to 0.1875
- land_mask: int32 [64], P('tile'), may hold values 0 or 1
- placement: int32 [64], replicated, may hold values from 0 to 63, as said below
- guide: bfloat16 [256, 256, 256], P(('tile', 'mp')), may hold values from -6 to 6
- conv_weights: bfloat16 [3, 3, 3, 256, 256], replicated, may hold values from -0.125 to 0.125
- conv_bias: float32 [3, 256], replicated, may hold values from -3 to 3
Outputs:
- dense_map: bfloat16 [256, 256, 256], P(('tile', 'mp'))
The draws below stay inside these ranges and needn't reach their ends.
Inputs may be any that keep to these rules, and one draw needn't show every extreme that they name: placement is a permutation of the scene positions; the tiles of one group land in different slabs (entry // 8), so each slab receives at most one tile of each group.
All inputs are finite; a program needn't handle non-finite values. No bound on the sum of `land_mask` on one device may be relied on, other than what follows from the above.
Results may differ from the reference program's by a relative error of at most 0.018.
The reference program's roundings to bfloat16 on the way count: a program that leaves them out, or rounds other values in their place, can miss the bound.
Values may be sent and summed in bfloat16 or wider, within the bound.
A program may use at most 128 MiB of HBM per device.

```python
import jax
import jax.numpy as jnp
from jax import lax

D = 1024
HEADS = 16
HEAD = 64
FF = 4096
SIDE = 16
C = 256
UP = 2
TILE_DEV = 8
PATCHES = 256
TILES = 64
PX_ROWS = 256
PX_COLS = 256
N_TILE = 8


def draw_tokens(key, part):
    key = jax.random.fold_in(key, 13)
    return jnp.clip(jax.random.normal(key, (TILES, PATCHES, D), jnp.float32), -6.0, 6.0).astype(jnp.bfloat16)


def draw_qkv_weight(key, part):
    key = jax.random.fold_in(key, 11)
    return (jnp.clip(jax.random.normal(key, (3, D, D), jnp.float32), -6.0, 6.0) * D ** (-0.5)).astype(jnp.bfloat16)


def draw_placement(key, part):
    key = jax.random.fold_in(key, 7)
    key_shift, key_offset, key_column = jax.random.split(key, 3)
    group_shift = jax.random.permutation(key_shift, N_TILE)
    offsets = jax.random.permutation(key_offset, N_TILE)[:TILE_DEV]
    tile_index = jnp.arange(TILES, dtype=jnp.int32)
    tile_group = tile_index // TILE_DEV
    within = tile_index % TILE_DEV
    slab_index = (group_shift[tile_group] + offsets[within]) % N_TILE
    scores = jax.random.randint(key_column, (N_TILE, TILE_DEV), 0, 1 << 20) * TILE_DEV + jnp.arange(TILE_DEV)[None, :]
    column_order = jnp.argsort(scores, axis=1)
    column = column_order[slab_index, within]
    return (slab_index * TILE_DEV + column).astype(jnp.int32)


def place_ends(drawn, stream_key, least, largest):
    longest = drawn.shape.index(max(drawn.shape))
    spots = []
    for shift in (0, 1):
        where = [jax.random.randint(jax.random.fold_in(stream_key, axis), (), 0, length) for axis, length in enumerate(drawn.shape)]
        where[longest] = (where[longest] + shift) % drawn.shape[longest]
        spots.append(tuple(where))
    return drawn.at[spots[0]].set(least).at[spots[1]].set(largest)


def shard_levels(own_key, extent, shards, least, largest):
    factor_of = 1.0
    for axis_at, shards_of in shards:
        draws = jax.random.uniform(jax.random.fold_in(jax.random.fold_in(own_key, 6), axis_at), (shards_of,), jnp.float32, least / len(shards), largest / len(shards))
        factor_of = factor_of * jnp.repeat(jnp.exp(draws), extent[axis_at] // shards_of).reshape((-1,) + (1,) * (len(extent) - 1 - axis_at))
    return factor_of


def noise(own_key, shape, scale, reach, shards=(), held_as=jnp.bfloat16):
    values = scale * jax.random.normal(own_key, shape, jnp.float32)
    if shards:
        values = values * shard_levels(own_key, shape, shards, -0.22, 0.18)
    return jnp.clip(values, -reach, reach).astype(held_as)


def setup_inputs(seed: int = 0) -> dict:
    keys = jax.random.split(jax.random.key(seed), 14)
    return {
        "tokens": draw_tokens(jax.random.fold_in(keys[13], 71), 0),
        "ln_gain_one": jnp.clip(1.0 + 0.1 * jax.random.normal(keys[1], (D,), jnp.float32), 0.5, 1.5),
        "ln_gain_two": jnp.clip(1.0 + 0.1 * jax.random.normal(keys[2], (D,), jnp.float32), 0.5, 1.5),
        "qkv_weight": draw_qkv_weight(jax.random.fold_in(keys[13], 71), 0),
        "out_weight": noise(keys[4], (D, D), D ** -0.5, 0.1875, ((0, 4),)),
        "in_weight": noise(keys[5], (FF, D), D ** -0.5, 0.1875, ((0, 4),)),
        "mlp_out_weight": noise(keys[6], (FF, D), FF ** -0.5, 0.09375, ((0, 4),)),
        "proj_weight": noise(keys[7], (D, C), D ** -0.5, 0.1875),
        "land_mask": place_ends((jax.random.randint(keys[8], (TILES,), 0, 4) < 3).astype(jnp.int32), jax.random.fold_in(keys[8], 1), 0, 1),
        "placement": draw_placement(jax.random.fold_in(keys[13], 71), 0),
        "guide": noise(keys[10], (PX_ROWS, PX_COLS, C), 1.0, 6.0, ((0, 32),)),
        "conv_weights": noise(keys[11], (3, 3, 3, C, C), (9 * C) ** -0.5, 0.125),
        "conv_bias": noise(keys[12], (3, C), 0.5, 3.0, (), jnp.float32),
    }


def layer_norm(values, gain):
    widened = values.astype(jnp.float32)
    centre = lax.optimization_barrier(jnp.mean(widened, axis=-1, keepdims=True))
    spread = lax.optimization_barrier(jnp.mean((widened - centre) ** 2, axis=-1, keepdims=True))
    return ((widened - centre) * lax.rsqrt(spread + 1e-06) * gain).astype(jnp.bfloat16)

def one_tile(tile_tokens, ln_gain_one, ln_gain_two, qkv_weight, out_weight, in_weight, mlp_out_weight):
    normed = layer_norm(tile_tokens, ln_gain_one)
    query = jnp.dot(normed, qkv_weight[0], preferred_element_type=jnp.float32).astype(jnp.bfloat16)
    keys_all = jnp.dot(normed, qkv_weight[1], preferred_element_type=jnp.float32).astype(jnp.bfloat16)
    values_all = jnp.dot(normed, qkv_weight[2], preferred_element_type=jnp.float32).astype(jnp.bfloat16)
    query = query.reshape(PATCHES, HEADS, HEAD).astype(jnp.float32)
    keys_all = keys_all.reshape(PATCHES, HEADS, HEAD).astype(jnp.float32)
    values_all = values_all.reshape(PATCHES, HEADS, HEAD).astype(jnp.float32)
    scores = jnp.einsum('phe,qhe->hpq', query, keys_all) * HEAD ** (-0.5)
    soft = jax.nn.softmax(scores, axis=-1).astype(jnp.bfloat16)
    context = jnp.einsum('hpq,qhe->phe', soft.astype(jnp.float32), values_all).astype(jnp.bfloat16).reshape(PATCHES, D)
    attention = jnp.dot(context, out_weight, preferred_element_type=jnp.float32)
    middle = (tile_tokens.astype(jnp.float32) + attention).astype(jnp.bfloat16)
    normed_mid = layer_norm(middle, ln_gain_two)
    hidden = jax.nn.gelu(jnp.dot(normed_mid, in_weight.T, preferred_element_type=jnp.float32)).astype(jnp.bfloat16)
    mlp_part = jnp.dot(hidden, mlp_out_weight, preferred_element_type=jnp.float32)
    return (middle.astype(jnp.float32) + mlp_part).astype(jnp.bfloat16)

def convolve(image, kernel, shift):
    result = lax.conv_general_dilated(image.astype(jnp.float32)[None], kernel.astype(jnp.float32), (1, 1), 'SAME', dimension_numbers=('NHWC', 'HWIO', 'NHWC'), precision=lax.Precision.HIGHEST)
    return result[0] + shift

def reference(tokens, ln_gain_one, ln_gain_two, qkv_weight, out_weight, in_weight, mlp_out_weight, proj_weight, land_mask, placement, guide, conv_weights, conv_bias):
    features = lax.map(lambda tile_tokens: one_tile(tile_tokens, ln_gain_one, ln_gain_two, qkv_weight, out_weight, in_weight, mlp_out_weight), tokens)
    embed = jnp.dot(features.reshape(TILES * PATCHES, D), proj_weight, preferred_element_type=jnp.float32)
    embed = embed.astype(jnp.bfloat16).reshape(TILES, PATCHES, C) * land_mask.astype(jnp.bfloat16)[:, None, None]
    inverse = jnp.zeros((TILES,), jnp.int32).at[placement].set(jnp.arange(TILES, dtype=jnp.int32))
    arranged = embed[inverse].reshape(TILES // TILE_DEV, TILE_DEV, SIDE, SIDE, C)
    scene_grid = jnp.transpose(arranged, (0, 2, 1, 3, 4)).reshape(PX_ROWS // UP, PX_COLS // UP, C)
    upsampled = jnp.repeat(jnp.repeat(scene_grid, UP, axis=0), UP, axis=1)
    guided = (upsampled.astype(jnp.float32) + guide.astype(jnp.float32)).astype(jnp.bfloat16)
    first = jax.nn.gelu(convolve(guided, conv_weights[0], conv_bias[0])).astype(jnp.bfloat16)
    second = jax.nn.gelu(convolve(first, conv_weights[1], conv_bias[1])).astype(jnp.bfloat16)
    return (guided.astype(jnp.float32) + convolve(second, conv_weights[2], conv_bias[2])).astype(jnp.bfloat16)
```

```python
import functools

import jax
import jax.numpy as jnp
from jax import lax
from jax.experimental import pallas as pl
from jax.experimental.pallas import tpu as pltpu
from jax.sharding import PartitionSpec as P

HEAD = 64
SIDE = 16
UP = 2
PATCHES = 256
HALO = 3
PLANE = 8
KINDS = 10


def layer_norm(values, gain):
    widened = values.astype(jnp.float32)
    centre = jnp.mean(widened, axis=-1, keepdims=True)
    spread = jnp.mean((widened - centre) ** 2, axis=-1, keepdims=True)
    return ((widened - centre) * lax.rsqrt(spread + 1e-06) * gain).astype(jnp.bfloat16)


def flip(index, bit):
    return index + bit - 2 * bit * (index // bit % 2)


def gather_kernel(
    count,
    tiles_each,
    tokens_ref,
    qkv_ref,
    out_ref,
    in_ref,
    mlp_ref,
    seq_ref,
    qkv_all,
    out_all,
    in_all,
    mlp_all,
    token_send,
    token_recv,
    own_sem,
    chain_send,
    send_sem,
    recv_sem,
):
    me_t = lax.axis_index("tile")
    me_z = lax.axis_index("mp")
    seg = tokens_ref.shape[1]
    shards = (qkv_ref, out_ref, in_ref, mlp_ref)
    gathered = (qkv_all, out_all, in_all, mlp_all)

    barrier = pltpu.get_barrier_semaphore()
    for bit in (1, 2, 4):
        pl.semaphore_signal(
            barrier, inc=1, device_id={"tile": flip(me_t, bit), "mp": me_z},
            device_id_type=pl.DeviceIdType.MESH,
        )
    for step in range(1, count):
        pl.semaphore_signal(
            barrier, inc=1, device_id={"tile": me_t, "mp": lax.rem(me_z + step, count)},
            device_id_type=pl.DeviceIdType.MESH,
        )
    pl.semaphore_wait(barrier, 3 + count - 1)

    def piece(which, origin, owner, part=None):
        rows = gathered[which].shape[1] // PLANE
        cols = gathered[which].shape[2]
        begin = pl.multiple_of(owner % PLANE * rows, rows)
        if part is None:
            return (origin, pl.ds(begin, rows))
        if rows % 32 == 0:
            half = rows // 2
            return (origin, pl.ds(pl.multiple_of(begin + part * half, half), half))
        half = cols // 2
        return (origin, pl.ds(begin, rows), pl.ds(part * half, half))

    def remote(src, dst, send, recv, tile, mp):
        return pltpu.make_async_remote_copy(
            src_ref=src, dst_ref=dst, send_sem=send, recv_sem=recv,
            device_id={"tile": tile, "mp": mp}, device_id_type=pl.DeviceIdType.MESH,
        )

    token_copies = []
    for step in range(1, count):
        target = lax.rem(me_z + step, count)
        copy = remote(
            tokens_ref.at[pl.ds(target * tiles_each, tiles_each)],
            seq_ref.at[:, pl.ds(pl.multiple_of(me_z * seg, seg), seg)],
            token_send.at[step], token_recv.at[step], me_t, target,
        )
        copy.start()
        token_copies.append(copy)
    own_tokens = pltpu.make_async_copy(
        tokens_ref.at[pl.ds(me_z * tiles_each, tiles_each)],
        seq_ref.at[:, pl.ds(pl.multiple_of(me_z * seg, seg), seg)],
        token_send.at[0],
    )
    own_tokens.start()

    def chain(which, origin, src, up):
        slot = 1 if up else 0
        target = me_z + 1 if up else me_z - 1
        ref = src
        return remote(
            ref, gathered[which].at[piece(which, origin, me_t)],
            chain_send.at[which, origin, slot], recv_sem.at[which, origin, 0], me_t, target,
        )

    def own_piece(which):
        rows = shards[which].shape[0] // PLANE
        return shards[which].at[pl.ds(pl.multiple_of(me_t % PLANE * rows, rows), rows)]

    def first_sends(which, wait):
        for up in (True, False):
            @pl.when(me_z + 1 < count if up else me_z > 0)
            def _():
                copy = chain(which, me_z, own_piece(which), up)
                if wait:
                    copy.wait_send()
                else:
                    copy.start()

    def source(index):
        below, above = me_z, count - 1 - me_z
        least = jnp.minimum(below, above)
        paired = index < 2 * least
        down_side = jnp.where(paired, index % 2 == 0, below > above)
        far = jnp.where(paired, index // 2 + 1, index - least + 1)
        return jnp.where(down_side, me_z - far, me_z + far), down_side

    def ring(which, origin, owner, kind, part, bit):
        where = piece(which, origin, owner, part)
        ref = gathered[which].at[where]
        return remote(
            ref, ref, send_sem.at[which, origin, kind], recv_sem.at[which, origin, kind],
            flip(me_t, bit), me_z,
        )

    x_of, y_of = flip(me_t, 2), flip(me_t, 4)
    both = flip(x_of, 4)
    outward = {
        1: (me_t, None, 2),
        2: (me_t, None, 4),
        3: (x_of, 0, 4),
        4: (y_of, 1, 2),
        5: (me_t, None, 1),
        6: (x_of, None, 1),
        7: (y_of, None, 1),
        8: (both, 0, 1),
        9: (both, 1, 1),
    }

    def go(which, origin, kind):
        owner, part, bit = outward[kind]
        ring(which, origin, owner, kind, part, bit).start()

    def arrived(which, origin, kind):
        owner, part, bit = outward[kind]
        mirrored = flip(owner, bit)
        ring(which, origin, mirrored, kind, part, bit).wait_recv()

    def stage_a(which, index):
        origin, down_side = source(index)
        chain(which, origin, gathered[which].at[piece(which, origin, me_t)], True).wait_recv()
        for up in (True, False):
            @pl.when((down_side & (me_z + 1 < count)) if up else
                     (jnp.logical_not(down_side) & (me_z > 0)))
            def _():
                chain(which, origin, gathered[which].at[piece(which, origin, me_t)], up).start()
        go(which, origin, 1)
        go(which, origin, 2)
        go(which, origin, 5)

    def stage_b(which, index):
        origin, _ = source(index)
        arrived(which, origin, 1)
        go(which, origin, 3)
        go(which, origin, 6)
        arrived(which, origin, 2)
        go(which, origin, 4)
        go(which, origin, 7)

    def stage_c(which, index):
        origin, _ = source(index)
        arrived(which, origin, 3)
        go(which, origin, 8)
        arrived(which, origin, 4)
        go(which, origin, 9)

    def stage_d(which, index):
        origin, _ = source(index)
        for kind in (5, 6, 7, 8, 9):
            arrived(which, origin, kind)

    own_copies = [
        pltpu.make_async_copy(shards[which], gathered[which].at[me_z], own_sem.at[which])
        for which in range(4)
    ]
    first_sends(0, False)
    for copy in own_copies:
        copy.start()
    first_sends(1, False)

    units = [(which, index) for which in range(4) for index in range(count - 1)]
    stages = (stage_a, stage_b, stage_c, stage_d)
    for tick in range(len(units) + 3):
        for late, stage in enumerate(stages):
            at = tick - late
            if 0 <= at < len(units):
                stage(*units[at])
                if late == 0 and units[at][1] == 0 and units[at][0] + 2 < 4:
                    first_sends(units[at][0] + 2, False)

    own_tokens.wait()
    for copy in token_copies:
        copy.wait()
    for copy in own_copies:
        copy.wait()
    for which in range(4):
        first_sends(which, True)
        for index in range(count - 1):
            origin, down_side = source(index)
            for up in (True, False):
                @pl.when((down_side & (me_z + 1 < count)) if up else
                         (jnp.logical_not(down_side) & (me_z > 0)))
                def _():
                    chain(
                        which, origin, gathered[which].at[piece(which, origin, me_t)], up
                    ).wait_send()
            for kind in range(1, KINDS):
                owner, part, bit = outward[kind]
                ring(which, origin, owner, kind, part, bit).wait_send()


def gather_all(tokens, qkv, out, into, mlp):
    count = lax.axis_size("mp")
    tiles_each = tokens.shape[0] // count
    any_space = pl.BlockSpec(memory_space=pl.ANY)
    return pl.pallas_call(
        functools.partial(gather_kernel, count, tiles_each),
        out_shape=(
            jax.ShapeDtypeStruct((tiles_each, PATCHES, tokens.shape[2]), jnp.bfloat16),
        ) + tuple(
            jax.ShapeDtypeStruct((count,) + part.shape, jnp.bfloat16)
            for part in (qkv, out, into, mlp)
        ),
        in_specs=[any_space] * 5,
        out_specs=(any_space,) * 5,
        scratch_shapes=[
            pltpu.SemaphoreType.DMA((count,)),
            pltpu.SemaphoreType.DMA((count,)),
            pltpu.SemaphoreType.DMA((4,)),
            pltpu.SemaphoreType.DMA((4, count, 2)),
            pltpu.SemaphoreType.DMA((4, count, KINDS)),
            pltpu.SemaphoreType.DMA((4, count, KINDS)),
        ],
        compiler_params=pltpu.CompilerParams(collective_id=0, has_side_effects=True),
        name="gather_weights",
    )(tokens, qkv, out, into, mlp)


def neighbours(block, width):
    axes = ("tile", "mp")
    count = lax.axis_size(axes)
    forward = [(i, i + 1) for i in range(count - 1)]
    backward = [(target, source) for source, target in forward]
    low = lax.ppermute(block[block.shape[0] - width:], axes, forward)
    high = lax.ppermute(block[:width], axes, backward)
    return low, high


def conv_layer(extended, kernel, shift, out_count):
    width_px = extended.shape[1]
    padded = jnp.pad(extended, ((0, 0), (1, 1), (0, 0)))
    running = jnp.zeros((out_count, width_px, kernel.shape[-1]), jnp.float32) + shift
    for row_shift in range(3):
        for col_shift in range(3):
            window = padded[row_shift : row_shift + out_count, col_shift : col_shift + width_px]
            running = running + jnp.einsum(
                "rwc,cd->rwd",
                window,
                kernel[row_shift, col_shift],
                preferred_element_type=jnp.float32,
            )
    return running


def per_device(
    tokens,
    ln_gain_one,
    ln_gain_two,
    qkv_weight,
    out_weight,
    in_weight,
    mlp_out_weight,
    proj_weight,
    land_mask,
    placement,
    guide,
    conv_weights,
    conv_bias,
):
    tiles_here, seg_rows, width = tokens.shape
    groups = lax.axis_size("tile")
    parts = lax.axis_size("mp")
    tiles_each = tiles_here // parts
    here = lax.axis_index(("tile", "mp"))
    guide_low, guide_high = neighbours(guide, HALO)

    heads_local = qkv_weight.shape[2] // HEAD
    seq, qkv_all, out_all, in_all, mlp_all = gather_all(
        tokens, qkv_weight.reshape(-1, qkv_weight.shape[2]), out_weight, in_weight, mlp_out_weight
    )
    qkv_all = qkv_all.reshape(parts, 3, width, heads_local * HEAD)
    out_all = out_all.reshape(-1, width)
    in_all = in_all.reshape(-1, width)
    mlp_all = mlp_all.reshape(-1, width)

    normed = layer_norm(seq, ln_gain_one)
    projected = jnp.einsum(
        "tpd,zkde->kztpe", normed, qkv_all, preferred_element_type=jnp.float32
    ).astype(jnp.bfloat16)
    shaped = projected.reshape(3, parts, tiles_each, PATCHES, heads_local, HEAD)
    scores = jnp.einsum(
        "ztphe,ztqhe->zthpq", shaped[0], shaped[1], preferred_element_type=jnp.float32
    ) * HEAD ** (-0.5)
    soft_weights = jax.nn.softmax(scores, axis=-1).astype(jnp.bfloat16)
    context = jnp.einsum(
        "zthpq,ztqhe->tpzhe", soft_weights, shaped[2], preferred_element_type=jnp.float32
    )
    context = context.astype(jnp.bfloat16).reshape(tiles_each, PATCHES, width)
    attention = jnp.einsum("tpe,ed->tpd", context, out_all, preferred_element_type=jnp.float32)
    middle = (seq.astype(jnp.float32) + attention).astype(jnp.bfloat16)
    normed_mid = layer_norm(middle, ln_gain_two)
    hidden = jnp.einsum("tpd,fd->tpf", normed_mid, in_all, preferred_element_type=jnp.float32)
    hidden = jax.nn.gelu(hidden).astype(jnp.bfloat16)
    mlp_part = jnp.einsum("tpf,fd->tpd", hidden, mlp_all, preferred_element_type=jnp.float32)
    features = (middle.astype(jnp.float32) + mlp_part).astype(jnp.bfloat16)
    mask_here = lax.dynamic_slice_in_dim(
        land_mask, lax.axis_index("mp") * tiles_each, tiles_each, 0
    ).astype(jnp.bfloat16)
    embed = jnp.einsum("tpd,dc->tpc", features, proj_weight, preferred_element_type=jnp.float32)
    embed = embed.astype(jnp.bfloat16) * mask_here[:, None, None]
    channels = embed.shape[-1]

    split = embed.reshape(tiles_each, parts, seg_rows, channels).transpose(1, 0, 2, 3)
    split = lax.all_to_all(split, "mp", split_axis=0, concat_axis=0, tiled=True)
    split = split.reshape(tiles_here, seg_rows, channels)

    group_here = lax.axis_index("tile")
    slab_all = placement // tiles_here
    column_all = placement % tiles_here
    group_all = jnp.arange(placement.shape[0], dtype=jnp.int32) // tiles_here
    slab_local = lax.dynamic_slice_in_dim(slab_all, group_here * tiles_here, tiles_here, 0)
    selector = (slab_local[None, :] == jnp.arange(groups, dtype=jnp.int32)[:, None]).astype(
        jnp.bfloat16
    )
    in_slab = slab_all == group_here
    column_hot = (
        column_all[:, None] == jnp.arange(tiles_here, dtype=jnp.int32)[None, :]
    ) & in_slab[:, None]
    group_hot = group_all[:, None] == jnp.arange(groups, dtype=jnp.int32)[None, :]
    arrange = jnp.einsum(
        "tk,tg->kg", column_hot.astype(jnp.float32), group_hot.astype(jnp.float32)
    ).astype(jnp.bfloat16)
    outgoing = jnp.einsum(
        "sj,jpd->spd", selector, split, preferred_element_type=jnp.float32
    ).astype(jnp.bfloat16)
    incoming = lax.all_to_all(outgoing, "tile", split_axis=0, concat_axis=0, tiled=True)
    slab_embed = jnp.einsum(
        "kg,gpd->kpd", arrange, incoming, preferred_element_type=jnp.float32
    ).astype(jnp.bfloat16)
    token_rows = seg_rows // SIDE
    image = slab_embed.reshape(tiles_here, token_rows, SIDE, channels)
    image = jnp.transpose(image, (1, 0, 2, 3)).reshape(token_rows, tiles_here * SIDE, channels)
    rows_low, rows_high = neighbours(image, UP)
    image = jnp.concatenate([rows_low, image, rows_high], axis=0)
    upsampled = jnp.repeat(jnp.repeat(image, UP, axis=0), UP, axis=1)[1:-1]
    guide_wide = jnp.concatenate([guide_low, guide, guide_high], axis=0)
    guided = (upsampled.astype(jnp.float32) + guide_wide.astype(jnp.float32)).astype(jnp.bfloat16)
    row_count = guide.shape[0]
    scene_rows = row_count * groups * parts

    def inside(values, reach):
        row = here * row_count - reach + jnp.arange(values.shape[0], dtype=jnp.int32)
        keep = (row >= 0) & (row < scene_rows)
        return jnp.where(keep[:, None, None], values, jnp.zeros((), values.dtype))

    def section(values, layer):
        return conv_layer(values, conv_weights[layer], conv_bias[layer], values.shape[0] - 2)

    first = inside(jax.nn.gelu(section(guided, 0)).astype(jnp.bfloat16), 2)
    second = inside(jax.nn.gelu(section(first, 1)).astype(jnp.bfloat16), 1)
    last_term = section(second, 2)
    return (guided[HALO:-HALO].astype(jnp.float32) + last_term).astype(jnp.bfloat16)


def solution(mesh):
    in_specs = (
        P("tile", "mp", None),
        P(),
        P(),
        P(None, None, "mp"),
        P("mp", None),
        P("mp", None),
        P("mp", None),
        P(),
        P("tile"),
        P(),
        P(("tile", "mp"), None, None),
        P(),
        P(),
    )
    out_specs = P(("tile", "mp"), None, None)
    return jax.shard_map(
        per_device, mesh=mesh, in_specs=in_specs, out_specs=out_specs, check_vma=False
    )
```

```python
import functools

import jax
import jax.numpy as jnp
from jax import lax
from jax.experimental import pallas as pl
from jax.experimental.pallas import tpu as pltpu
from jax.sharding import PartitionSpec as P

HEAD = 64
SIDE = 16
UP = 2
PATCHES = 256
HALO = 3
PLANE = 8
KINDS = 10


def layer_norm(values, gain):
    widened = values.astype(jnp.float32)
    centre = jnp.mean(widened, axis=-1, keepdims=True)
    spread = jnp.mean((widened - centre) ** 2, axis=-1, keepdims=True)
    return ((widened - centre) * lax.rsqrt(spread + 1e-06) * gain).astype(jnp.bfloat16)


def flip(index, bit):
    return index + bit - 2 * bit * (index // bit % 2)


def gather_kernel(
    count,
    tiles_each,
    tokens_ref,
    qkv_ref,
    out_ref,
    in_ref,
    mlp_ref,
    seq_ref,
    qkv_all,
    out_all,
    in_all,
    mlp_all,
    token_send,
    token_recv,
    own_sem,
    chain_send,
    send_sem,
    recv_sem,
):
    me_t = lax.axis_index("tile")
    me_z = lax.axis_index("mp")
    seg = tokens_ref.shape[1]
    shards = (qkv_ref, out_ref, in_ref, mlp_ref)
    gathered = (qkv_all, out_all, in_all, mlp_all)

    barrier = pltpu.get_barrier_semaphore()
    for bit in (1, 2, 4):
        pl.semaphore_signal(
            barrier, inc=1, device_id={"tile": flip(me_t, bit), "mp": me_z},
            device_id_type=pl.DeviceIdType.MESH,
        )
    for step in range(1, count):
        pl.semaphore_signal(
            barrier, inc=1, device_id={"tile": me_t, "mp": lax.rem(me_z + step, count)},
            device_id_type=pl.DeviceIdType.MESH,
        )
    pl.semaphore_wait(barrier, 3 + count - 1)

    def piece(which, origin, owner, part=None):
        rows = gathered[which].shape[1] // PLANE
        cols = gathered[which].shape[2]
        begin = pl.multiple_of(owner % PLANE * rows, rows)
        if part is None:
            return (origin, pl.ds(begin, rows))
        if rows % 32 == 0:
            half = rows // 2
            return (origin, pl.ds(pl.multiple_of(begin + part * half, half), half))
        half = cols // 2
        return (origin, pl.ds(begin, rows), pl.ds(part * half, half))

    def remote(src, dst, send, recv, tile, mp):
        return pltpu.make_async_remote_copy(
            src_ref=src, dst_ref=dst, send_sem=send, recv_sem=recv,
            device_id={"tile": tile, "mp": mp}, device_id_type=pl.DeviceIdType.MESH,
        )

    token_copies = []
    for step in range(1, count):
        target = lax.rem(me_z + step, count)
        copy = remote(
            tokens_ref.at[pl.ds(target * tiles_each, tiles_each)],
            seq_ref.at[:, pl.ds(pl.multiple_of(me_z * seg, seg), seg)],
            token_send.at[step], token_recv.at[step], me_t, target,
        )
        copy.start()
        token_copies.append(copy)
    own_tokens = pltpu.make_async_copy(
        tokens_ref.at[pl.ds(me_z * tiles_each, tiles_each)],
        seq_ref.at[:, pl.ds(pl.multiple_of(me_z * seg, seg), seg)],
        token_send.at[0],
    )
    own_tokens.start()

    def chain(which, origin, src, up):
        slot = 1 if up else 0
        target = me_z + 1 if up else me_z - 1
        ref = src
        return remote(
            ref, gathered[which].at[piece(which, origin, me_t)],
            chain_send.at[which, origin, slot], recv_sem.at[which, origin, 0], me_t, target,
        )

    def own_piece(which):
        rows = shards[which].shape[0] // PLANE
        return shards[which].at[pl.ds(pl.multiple_of(me_t % PLANE * rows, rows), rows)]

    def first_sends(which, wait):
        for up in (True, False):
            @pl.when(me_z + 1 < count if up else me_z > 0)
            def _():
                copy = chain(which, me_z, own_piece(which), up)
                if wait:
                    copy.wait_send()
                else:
                    copy.start()

    def source(index):
        below, above = me_z, count - 1 - me_z
        least = jnp.minimum(below, above)
        paired = index < 2 * least
        down_side = jnp.where(paired, index % 2 == 0, below > above)
        far = jnp.where(paired, index // 2 + 1, index - least + 1)
        return jnp.where(down_side, me_z - far, me_z + far), down_side

    def ring(which, origin, owner, kind, part, bit):
        where = piece(which, origin, owner, part)
        ref = gathered[which].at[where]
        return remote(
            ref, ref, send_sem.at[which, origin, kind], recv_sem.at[which, origin, kind],
            flip(me_t, bit), me_z,
        )

    def routes(device):
        first_bit = 2 + 2 * (device % 2)
        second_bit = 4 - 2 * (device % 2)
        first_of, second_of = flip(device, first_bit), flip(device, second_bit)
        both = flip(flip(device, 2), 4)
        return {
            1: (device, None, first_bit),
            2: (device, None, second_bit),
            3: (first_of, 0, second_bit),
            4: (second_of, 1, first_bit),
            5: (device, None, 1),
            6: (first_of, None, 1),
            7: (second_of, None, 1),
            8: (both, 0, 1),
            9: (both, 1, 1),
        }

    outward = routes(me_t)
    inward = routes(flip(me_t, 1))

    def go(which, origin, kind):
        owner, part, bit = outward[kind]
        ring(which, origin, owner, kind, part, bit).start()

    def arrived(which, origin, kind):
        owner, part, bit = (outward if kind < 5 else inward)[kind]
        if kind < 5:
            owner = flip(owner, bit)
        ring(which, origin, owner, kind, part, bit).wait_recv()

    def stage_a(which, index):
        origin, down_side = source(index)
        chain(which, origin, gathered[which].at[piece(which, origin, me_t)], True).wait_recv()
        for up in (True, False):
            @pl.when((down_side & (me_z + 1 < count)) if up else
                     (jnp.logical_not(down_side) & (me_z > 0)))
            def _():
                chain(which, origin, gathered[which].at[piece(which, origin, me_t)], up).start()
        go(which, origin, 1)
        go(which, origin, 2)
        go(which, origin, 5)

    def stage_b(which, index):
        origin, _ = source(index)
        arrived(which, origin, 1)
        go(which, origin, 3)
        go(which, origin, 6)
        arrived(which, origin, 2)
        go(which, origin, 4)
        go(which, origin, 7)

    def stage_c(which, index):
        origin, _ = source(index)
        arrived(which, origin, 3)
        go(which, origin, 8)
        arrived(which, origin, 4)
        go(which, origin, 9)

    def stage_d(which, index):
        origin, _ = source(index)
        for kind in (5, 6, 7, 8, 9):
            arrived(which, origin, kind)

    own_copies = [
        pltpu.make_async_copy(shards[which], gathered[which].at[me_z], own_sem.at[which])
        for which in range(4)
    ]
    first_sends(0, False)
    for copy in own_copies:
        copy.start()
    first_sends(1, False)

    units = [(which, index) for which in range(4) for index in range(count - 1)]
    stages = (stage_a, stage_b, stage_c)
    for tick in range(len(units) + 2):
        for late, stage in enumerate(stages):
            at = tick - late
            if 0 <= at < len(units):
                stage(*units[at])
                if late == 0 and units[at][1] == 0 and units[at][0] + 2 < 4:
                    first_sends(units[at][0] + 2, False)

    for which, index in units:
        stage_d(which, index)
    own_tokens.wait()
    for copy in token_copies:
        copy.wait()
    for copy in own_copies:
        copy.wait()
    for which in range(4):
        first_sends(which, True)
        for index in range(count - 1):
            origin, down_side = source(index)
            for up in (True, False):
                @pl.when((down_side & (me_z + 1 < count)) if up else
                         (jnp.logical_not(down_side) & (me_z > 0)))
                def _():
                    chain(
                        which, origin, gathered[which].at[piece(which, origin, me_t)], up
                    ).wait_send()
            for kind in range(1, KINDS):
                owner, part, bit = outward[kind]
                ring(which, origin, owner, kind, part, bit).wait_send()


def gather_all(tokens, qkv, out, into, mlp):
    count = lax.axis_size("mp")
    tiles_each = tokens.shape[0] // count
    any_space = pl.BlockSpec(memory_space=pl.ANY)
    return pl.pallas_call(
        functools.partial(gather_kernel, count, tiles_each),
        out_shape=(
            jax.ShapeDtypeStruct((tiles_each, PATCHES, tokens.shape[2]), jnp.bfloat16),
        ) + tuple(
            jax.ShapeDtypeStruct((count,) + part.shape, jnp.bfloat16)
            for part in (qkv, out, into, mlp)
        ),
        in_specs=[any_space] * 5,
        out_specs=(any_space,) * 5,
        scratch_shapes=[
            pltpu.SemaphoreType.DMA((count,)),
            pltpu.SemaphoreType.DMA((count,)),
            pltpu.SemaphoreType.DMA((4,)),
            pltpu.SemaphoreType.DMA((4, count, 2)),
            pltpu.SemaphoreType.DMA((4, count, KINDS)),
            pltpu.SemaphoreType.DMA((4, count, KINDS)),
        ],
        compiler_params=pltpu.CompilerParams(collective_id=0, has_side_effects=True),
        name="gather_weights",
    )(tokens, qkv, out, into, mlp)


def neighbours(block, width, dim=0):
    axes = ("tile", "mp")
    count = lax.axis_size(axes)
    forward = [(i, i + 1) for i in range(count - 1)]
    backward = [(target, source) for source, target in forward]
    low = lax.ppermute(lax.slice_in_dim(block, block.shape[dim] - width, None, axis=dim), axes, forward)
    high = lax.ppermute(lax.slice_in_dim(block, 0, width, axis=dim), axes, backward)
    return low, high


def scene_kernel(
    row_count,
    scene_rows,
    low_ref,
    mid_ref,
    high_ref,
    guide_low,
    guide_mid,
    guide_high,
    weights_ref,
    bias_ref,
    result_ref,
    guided_buf,
    first_buf,
    second_buf,
):
    here = lax.axis_index(("tile", "mp"))
    width_px, channels = guide_mid.shape[1:]
    cols = width_px // UP
    column = lax.broadcasted_iota(jnp.int32, (width_px, channels), 0)
    spread = (
        lax.broadcasted_iota(jnp.int32, (width_px, cols), 0) // UP
        == lax.broadcasted_iota(jnp.int32, (width_px, cols), 1)
    ).astype(jnp.bfloat16)

    def put(buffer, row, values):
        before = jnp.where(column == 0, 0.0, pltpu.roll(values, 1, 0))
        after = jnp.where(column == width_px - 1, 0.0, pltpu.roll(values, width_px - 1, 0))
        buffer[row, :, pl.ds(0, channels)] = before.astype(jnp.bfloat16)
        buffer[row, :, pl.ds(channels, channels)] = values.astype(jnp.bfloat16)
        buffer[row, :, pl.ds(2 * channels, channels)] = after.astype(jnp.bfloat16)

    def token_row(row):
        inner = mid_ref.shape[1] // SIDE
        if row < UP:
            ref, at = low_ref, row
        elif row < UP + inner:
            ref, at = mid_ref, row - UP
        else:
            ref, at = high_ref, row - UP - inner
        line = ref[:, pl.ds(at * SIDE, SIDE), :].reshape(cols, channels)
        return jnp.dot(spread, line, preferred_element_type=jnp.float32)

    def guide_row(row):
        if row < HALO:
            return guide_low[row]
        if row < HALO + row_count:
            return guide_mid[row - HALO]
        return guide_high[row - HALO - row_count]

    for row in range(row_count + 2 * HALO):
        put(guided_buf, row, token_row((row + 1) // UP) + guide_row(row).astype(jnp.float32))

    def conv(buffer, layer, row):
        total = jnp.zeros((2 * width_px, channels), jnp.float32) + bias_ref[pl.ds(layer, 1), :]
        for shift in range(3):
            window = buffer[pl.ds(row + shift, 2)].reshape(2 * width_px, 3 * channels)
            total += jnp.dot(window, weights_ref[layer, shift], preferred_element_type=jnp.float32)
        return total

    for layer, source, target in ((0, guided_buf, first_buf), (1, first_buf, second_buf)):
        reach = HALO - 1 - layer

        @pl.loop(0, row_count // 2 + reach)
        def _(pair):
            values = jax.nn.gelu(conv(source, layer, 2 * pair))
            for part in range(2):
                at = here * row_count - reach + 2 * pair + part
                keep = (at >= 0) & (at < scene_rows)
                line = values[part * width_px : (part + 1) * width_px]
                put(target, 2 * pair + part, jnp.where(keep, line, 0.0))

    @pl.loop(0, row_count // 2)
    def _(pair):
        values = conv(second_buf, 2, 2 * pair).reshape(2, width_px, channels)
        base = guided_buf[pl.ds(2 * pair + HALO, 2), :, pl.ds(channels, channels)]
        result_ref[pl.ds(2 * pair, 2)] = (base.astype(jnp.float32) + values).astype(jnp.bfloat16)


def scene(slab, guide, guide_low, guide_high, conv_weights, conv_bias):
    rows, width_px, channels = guide.shape
    ring = lax.axis_size(("tile", "mp"))
    low, high = neighbours(slab, UP * SIDE, 1)
    weights = conv_weights.reshape(3, 3, 3 * channels, channels)
    return pl.pallas_call(
        functools.partial(scene_kernel, rows, rows * ring),
        out_shape=jax.ShapeDtypeStruct(guide.shape, jnp.bfloat16),
        in_specs=[pl.BlockSpec(memory_space=pltpu.VMEM)] * 8,
        out_specs=pl.BlockSpec(memory_space=pltpu.VMEM),
        scratch_shapes=[
            pltpu.VMEM((rows + 2 * reach, width_px, 3 * channels), jnp.bfloat16)
            for reach in (3, 2, 1)
        ],
        compiler_params=pltpu.CompilerParams(vmem_limit_bytes=50 << 20),
        name="scene_convolutions",
    )(low, slab, high, guide_low, guide, guide_high, weights, conv_bias)


def per_device(
    tokens,
    ln_gain_one,
    ln_gain_two,
    qkv_weight,
    out_weight,
    in_weight,
    mlp_out_weight,
    proj_weight,
    land_mask,
    placement,
    guide,
    conv_weights,
    conv_bias,
):
    tiles_here, seg_rows, width = tokens.shape
    groups = lax.axis_size("tile")
    parts = lax.axis_size("mp")
    tiles_each = tiles_here // parts
    guide_low, guide_high = neighbours(guide, HALO)

    heads_local = qkv_weight.shape[2] // HEAD
    seq, qkv_all, out_all, in_all, mlp_all = gather_all(
        tokens, qkv_weight.reshape(-1, qkv_weight.shape[2]), out_weight, in_weight, mlp_out_weight
    )
    qkv_all = qkv_all.reshape(parts, 3, width, heads_local * HEAD)
    out_all = out_all.reshape(-1, width)
    in_all = in_all.reshape(-1, width)
    mlp_all = mlp_all.reshape(-1, width)

    normed = layer_norm(seq, ln_gain_one)
    projected = jnp.einsum(
        "tpd,zkde->kztpe", normed, qkv_all, preferred_element_type=jnp.float32
    ).astype(jnp.bfloat16)
    shaped = projected.reshape(3, parts, tiles_each, PATCHES, heads_local, HEAD)
    scores = jnp.einsum(
        "ztphe,ztqhe->zthpq", shaped[0], shaped[1], preferred_element_type=jnp.float32
    ) * HEAD ** (-0.5)
    soft_weights = jax.nn.softmax(scores, axis=-1).astype(jnp.bfloat16)
    context = jnp.einsum(
        "zthpq,ztqhe->tpzhe", soft_weights, shaped[2], preferred_element_type=jnp.float32
    )
    context = context.astype(jnp.bfloat16).reshape(tiles_each, PATCHES, width)
    attention = jnp.einsum("tpe,ed->tpd", context, out_all, preferred_element_type=jnp.float32)
    middle = (seq.astype(jnp.float32) + attention).astype(jnp.bfloat16)
    normed_mid = layer_norm(middle, ln_gain_two)
    hidden = jnp.einsum("tpd,fd->tpf", normed_mid, in_all, preferred_element_type=jnp.float32)
    hidden = jax.nn.gelu(hidden).astype(jnp.bfloat16)
    mlp_part = jnp.einsum("tpf,fd->tpd", hidden, mlp_all, preferred_element_type=jnp.float32)
    features = (middle.astype(jnp.float32) + mlp_part).astype(jnp.bfloat16)
    mask_here = lax.dynamic_slice_in_dim(
        land_mask, lax.axis_index("mp") * tiles_each, tiles_each, 0
    ).astype(jnp.bfloat16)
    embed = jnp.einsum("tpd,dc->tpc", features, proj_weight, preferred_element_type=jnp.float32)
    embed = embed.astype(jnp.bfloat16) * mask_here[:, None, None]
    channels = embed.shape[-1]

    split = embed.reshape(tiles_each, parts, seg_rows, channels).transpose(1, 0, 2, 3)
    split = lax.all_to_all(split, "mp", split_axis=0, concat_axis=0, tiled=True)
    split = split.reshape(tiles_here, seg_rows, channels)

    group_here = lax.axis_index("tile")
    slab_all = placement // tiles_here
    column_all = placement % tiles_here
    group_all = jnp.arange(placement.shape[0], dtype=jnp.int32) // tiles_here
    slab_local = lax.dynamic_slice_in_dim(slab_all, group_here * tiles_here, tiles_here, 0)
    selector = (slab_local[None, :] == jnp.arange(groups, dtype=jnp.int32)[:, None]).astype(
        jnp.bfloat16
    )
    in_slab = slab_all == group_here
    column_hot = (
        column_all[:, None] == jnp.arange(tiles_here, dtype=jnp.int32)[None, :]
    ) & in_slab[:, None]
    group_hot = group_all[:, None] == jnp.arange(groups, dtype=jnp.int32)[None, :]
    arrange = jnp.einsum(
        "tk,tg->kg", column_hot.astype(jnp.float32), group_hot.astype(jnp.float32)
    ).astype(jnp.bfloat16)
    outgoing = jnp.einsum(
        "sj,jpd->spd", selector, split, preferred_element_type=jnp.float32
    ).astype(jnp.bfloat16)
    incoming = lax.all_to_all(outgoing, "tile", split_axis=0, concat_axis=0, tiled=True)
    slab_embed = jnp.einsum(
        "kg,gpd->kpd", arrange, incoming, preferred_element_type=jnp.float32
    ).astype(jnp.bfloat16)
    return scene(slab_embed, guide, guide_low, guide_high, conv_weights, conv_bias)


def solution(mesh):
    in_specs = (
        P("tile", "mp", None),
        P(),
        P(),
        P(None, None, "mp"),
        P("mp", None),
        P("mp", None),
        P("mp", None),
        P(),
        P("tile"),
        P(),
        P(("tile", "mp"), None, None),
        P(),
        P(),
    )
    out_specs = P(("tile", "mp"), None, None)
    return jax.shard_map(
        per_device, mesh=mesh, in_specs=in_specs, out_specs=out_specs, check_vma=False
    )
```

```python
import functools

import jax
import jax.numpy as jnp
from jax import lax
from jax.experimental import pallas as pl
from jax.experimental.pallas import tpu as pltpu
from jax.sharding import PartitionSpec as P

HEAD = 64
SIDE = 16
UP = 2
PATCHES = 256
HALO = 3
PLANE = 8
KINDS = 10


def layer_norm(values, gain):
    widened = values.astype(jnp.float32)
    centre = jnp.mean(widened, axis=-1, keepdims=True)
    spread = jnp.mean((widened - centre) ** 2, axis=-1, keepdims=True)
    return ((widened - centre) * lax.rsqrt(spread + 1e-06) * gain).astype(jnp.bfloat16)


def flip(index, bit):
    return index + bit - 2 * bit * (index // bit % 2)


def gather_kernel(
    count,
    tiles_each,
    tokens_ref,
    qkv_ref,
    out_ref,
    in_ref,
    mlp_ref,
    seq_ref,
    qkv_all,
    out_all,
    in_all,
    mlp_all,
    token_send,
    token_recv,
    own_sem,
    chain_send,
    send_sem,
    recv_sem,
):
    me_t = lax.axis_index("tile")
    me_z = lax.axis_index("mp")
    seg = tokens_ref.shape[1]
    shards = (qkv_ref, out_ref, in_ref, mlp_ref)
    gathered = (qkv_all, out_all, in_all, mlp_all)

    barrier = pltpu.get_barrier_semaphore()
    for bit in (1, 2, 4):
        pl.semaphore_signal(
            barrier, inc=1, device_id={"tile": flip(me_t, bit), "mp": me_z},
            device_id_type=pl.DeviceIdType.MESH,
        )
    for step in range(1, count):
        pl.semaphore_signal(
            barrier, inc=1, device_id={"tile": me_t, "mp": lax.rem(me_z + step, count)},
            device_id_type=pl.DeviceIdType.MESH,
        )
    pl.semaphore_wait(barrier, 3 + count - 1)

    shared = (True, True, False, False)

    def piece(which, origin, owner, part=None):
        split = PLANE if shared[which] else PLANE // 2
        rows = gathered[which].shape[1] // split
        cols = gathered[which].shape[2]
        place = owner % PLANE if shared[which] else owner % PLANE // 2
        begin = pl.multiple_of(place * rows, rows)
        if part is None:
            return (origin, pl.ds(begin, rows))
        if rows % 32 == 0:
            half = rows // 2
            return (origin, pl.ds(pl.multiple_of(begin + part * half, half), half))
        half = cols // 2
        return (origin, pl.ds(begin, rows), pl.ds(part * half, half))

    def remote(src, dst, send, recv, tile, mp):
        return pltpu.make_async_remote_copy(
            src_ref=src, dst_ref=dst, send_sem=send, recv_sem=recv,
            device_id={"tile": tile, "mp": mp}, device_id_type=pl.DeviceIdType.MESH,
        )

    token_copies = []
    for step in range(1, count):
        target = lax.rem(me_z + step, count)
        copy = remote(
            tokens_ref.at[pl.ds(target * tiles_each, tiles_each)],
            seq_ref.at[:, pl.ds(pl.multiple_of(me_z * seg, seg), seg)],
            token_send.at[step], token_recv.at[step], me_t, target,
        )
        copy.start()
        token_copies.append(copy)
    own_tokens = pltpu.make_async_copy(
        tokens_ref.at[pl.ds(me_z * tiles_each, tiles_each)],
        seq_ref.at[:, pl.ds(pl.multiple_of(me_z * seg, seg), seg)],
        token_send.at[0],
    )
    own_tokens.start()

    def chain(which, origin, src, up):
        slot = 1 if up else 0
        target = me_z + 1 if up else me_z - 1
        ref = src
        return remote(
            ref, gathered[which].at[piece(which, origin, me_t)],
            chain_send.at[which, origin, slot], recv_sem.at[which, origin, 0], me_t, target,
        )

    def own_piece(which):
        rows = shards[which].shape[0] // PLANE
        place = me_t % PLANE
        if not shared[which]:
            place = place % 2 * (PLANE // 2) + place // 2
        return shards[which].at[pl.ds(pl.multiple_of(place * rows, rows), rows)]

    def own_part(which):
        if shared[which]:
            return shards[which]
        rows = shards[which].shape[0] // 2
        return shards[which].at[pl.ds(pl.multiple_of(me_t % 2 * rows, rows), rows)]

    def first_sends(which, wait):
        for up in (True, False):
            @pl.when(me_z + 1 < count if up else me_z > 0)
            def _():
                copy = chain(which, me_z, own_piece(which), up)
                if wait:
                    copy.wait_send()
                else:
                    copy.start()

    def source(index):
        below, above = me_z, count - 1 - me_z
        least = jnp.minimum(below, above)
        paired = index < 2 * least
        down_side = jnp.where(paired, index % 2 == 0, below > above)
        far = jnp.where(paired, index // 2 + 1, index - least + 1)
        return jnp.where(down_side, me_z - far, me_z + far), down_side

    def ring(which, origin, owner, kind, part, bit):
        where = piece(which, origin, owner, part)
        ref = gathered[which].at[where]
        return remote(
            ref, ref, send_sem.at[which, origin, kind], recv_sem.at[which, origin, kind],
            flip(me_t, bit), me_z,
        )

    def routes(device):
        first_bit = 2 + 2 * (device % 2)
        second_bit = 4 - 2 * (device % 2)
        first_of, second_of = flip(device, first_bit), flip(device, second_bit)
        both = flip(flip(device, 2), 4)
        return {
            1: (device, None, first_bit),
            2: (device, None, second_bit),
            3: (first_of, 0, second_bit),
            4: (second_of, 1, first_bit),
            5: (device, None, 1),
            6: (first_of, None, 1),
            7: (second_of, None, 1),
            8: (both, 0, 1),
            9: (both, 1, 1),
        }

    outward = routes(me_t)
    inward = routes(flip(me_t, 1))

    def go(which, origin, kind):
        owner, part, bit = outward[kind]
        ring(which, origin, owner, kind, part, bit).start()

    def arrived(which, origin, kind):
        owner, part, bit = (outward if kind < 5 else inward)[kind]
        if kind < 5:
            owner = flip(owner, bit)
        ring(which, origin, owner, kind, part, bit).wait_recv()

    def stage_a(which, index):
        origin, down_side = source(index)
        chain(which, origin, gathered[which].at[piece(which, origin, me_t)], True).wait_recv()
        for up in (True, False):
            @pl.when((down_side & (me_z + 1 < count)) if up else
                     (jnp.logical_not(down_side) & (me_z > 0)))
            def _():
                chain(which, origin, gathered[which].at[piece(which, origin, me_t)], up).start()
        go(which, origin, 1)
        go(which, origin, 2)
        if shared[which]:
            go(which, origin, 5)

    def stage_b(which, index):
        origin, _ = source(index)
        arrived(which, origin, 1)
        go(which, origin, 3)
        if shared[which]:
            go(which, origin, 6)
        arrived(which, origin, 2)
        go(which, origin, 4)
        if shared[which]:
            go(which, origin, 7)

    def stage_c(which, index):
        origin, _ = source(index)
        arrived(which, origin, 3)
        if shared[which]:
            go(which, origin, 8)
        arrived(which, origin, 4)
        if shared[which]:
            go(which, origin, 9)

    def stage_d(which, index):
        origin, _ = source(index)
        for kind in (5, 6, 7, 8, 9):
            arrived(which, origin, kind)

    own_copies = [
        pltpu.make_async_copy(own_part(which), gathered[which].at[me_z], own_sem.at[which])
        for which in range(4)
    ]
    first_sends(0, False)
    for copy in own_copies:
        copy.start()
    first_sends(1, False)

    units = [(which, index) for which in range(4) for index in range(count - 1)]
    stages = (stage_a, stage_b, stage_c)
    for tick in range(len(units) + 2):
        for late, stage in enumerate(stages):
            at = tick - late
            if 0 <= at < len(units):
                stage(*units[at])
                if late == 0 and units[at][1] == 0 and units[at][0] + 2 < 4:
                    first_sends(units[at][0] + 2, False)

    for which, index in units:
        if shared[which]:
            stage_d(which, index)
    own_tokens.wait()
    for copy in token_copies:
        copy.wait()
    for copy in own_copies:
        copy.wait()
    for which in range(4):
        first_sends(which, True)
        for index in range(count - 1):
            origin, down_side = source(index)
            for up in (True, False):
                @pl.when((down_side & (me_z + 1 < count)) if up else
                         (jnp.logical_not(down_side) & (me_z > 0)))
                def _():
                    chain(
                        which, origin, gathered[which].at[piece(which, origin, me_t)], up
                    ).wait_send()
            for kind in range(1, KINDS if shared[which] else 5):
                owner, part, bit = outward[kind]
                ring(which, origin, owner, kind, part, bit).wait_send()


def gather_all(tokens, qkv, out, into, mlp):
    count = lax.axis_size("mp")
    tiles_each = tokens.shape[0] // count
    any_space = pl.BlockSpec(memory_space=pl.ANY)
    return pl.pallas_call(
        functools.partial(gather_kernel, count, tiles_each),
        out_shape=(
            jax.ShapeDtypeStruct((tiles_each, PATCHES, tokens.shape[2]), jnp.bfloat16),
        ) + tuple(
            jax.ShapeDtypeStruct((count, part.shape[0] // cut, part.shape[1]), jnp.bfloat16)
            for part, cut in ((qkv, 1), (out, 1), (into, 2), (mlp, 2))
        ),
        in_specs=[any_space] * 5,
        out_specs=(any_space,) * 5,
        scratch_shapes=[
            pltpu.SemaphoreType.DMA((count,)),
            pltpu.SemaphoreType.DMA((count,)),
            pltpu.SemaphoreType.DMA((4,)),
            pltpu.SemaphoreType.DMA((4, count, 2)),
            pltpu.SemaphoreType.DMA((4, count, KINDS)),
            pltpu.SemaphoreType.DMA((4, count, KINDS)),
        ],
        compiler_params=pltpu.CompilerParams(collective_id=0, has_side_effects=True),
        name="gather_weights",
    )(tokens, qkv, out, into, mlp)


def neighbours(block, width, dim=0):
    axes = ("tile", "mp")
    count = lax.axis_size(axes)
    forward = [(i, i + 1) for i in range(count - 1)]
    backward = [(target, source) for source, target in forward]
    low = lax.ppermute(lax.slice_in_dim(block, block.shape[dim] - width, None, axis=dim), axes, forward)
    high = lax.ppermute(lax.slice_in_dim(block, 0, width, axis=dim), axes, backward)
    return low, high


def scene_kernel(
    row_count,
    scene_rows,
    low_ref,
    mid_ref,
    high_ref,
    guide_low,
    guide_mid,
    guide_high,
    weights_ref,
    bias_ref,
    result_ref,
    guided_buf,
    first_buf,
    second_buf,
):
    here = lax.axis_index(("tile", "mp"))
    width_px, channels = guide_mid.shape[1:]
    cols = width_px // UP
    column = lax.broadcasted_iota(jnp.int32, (width_px, channels), 0)
    spread = (
        lax.broadcasted_iota(jnp.int32, (width_px, cols), 0) // UP
        == lax.broadcasted_iota(jnp.int32, (width_px, cols), 1)
    ).astype(jnp.bfloat16)

    def put(buffer, row, values):
        before = jnp.where(column == 0, 0.0, pltpu.roll(values, 1, 0))
        after = jnp.where(column == width_px - 1, 0.0, pltpu.roll(values, width_px - 1, 0))
        buffer[row, :, pl.ds(0, channels)] = before.astype(jnp.bfloat16)
        buffer[row, :, pl.ds(channels, channels)] = values.astype(jnp.bfloat16)
        buffer[row, :, pl.ds(2 * channels, channels)] = after.astype(jnp.bfloat16)

    def token_row(row):
        inner = mid_ref.shape[1] // SIDE
        if row < UP:
            ref, at = low_ref, row
        elif row < UP + inner:
            ref, at = mid_ref, row - UP
        else:
            ref, at = high_ref, row - UP - inner
        line = ref[:, pl.ds(at * SIDE, SIDE), :].reshape(cols, channels)
        return jnp.dot(spread, line, preferred_element_type=jnp.float32)

    def guide_row(row):
        if row < HALO:
            return guide_low[row]
        if row < HALO + row_count:
            return guide_mid[row - HALO]
        return guide_high[row - HALO - row_count]

    for row in range(row_count + 2 * HALO):
        put(guided_buf, row, token_row((row + 1) // UP) + guide_row(row).astype(jnp.float32))

    def conv(buffer, layer, row):
        total = jnp.zeros((2 * width_px, channels), jnp.float32) + bias_ref[pl.ds(layer, 1), :]
        for shift in range(3):
            window = buffer[pl.ds(row + shift, 2)].reshape(2 * width_px, 3 * channels)
            total += jnp.dot(window, weights_ref[layer, shift], preferred_element_type=jnp.float32)
        return total

    for layer, source, target in ((0, guided_buf, first_buf), (1, first_buf, second_buf)):
        reach = HALO - 1 - layer

        @pl.loop(0, row_count // 2 + reach)
        def _(pair):
            values = jax.nn.gelu(conv(source, layer, 2 * pair))
            for part in range(2):
                at = here * row_count - reach + 2 * pair + part
                keep = (at >= 0) & (at < scene_rows)
                line = values[part * width_px : (part + 1) * width_px]
                put(target, 2 * pair + part, jnp.where(keep, line, 0.0))

    @pl.loop(0, row_count // 2)
    def _(pair):
        values = conv(second_buf, 2, 2 * pair).reshape(2, width_px, channels)
        base = guided_buf[pl.ds(2 * pair + HALO, 2), :, pl.ds(channels, channels)]
        result_ref[pl.ds(2 * pair, 2)] = (base.astype(jnp.float32) + values).astype(jnp.bfloat16)


def scene(slab, guide, guide_low, guide_high, conv_weights, conv_bias):
    rows, width_px, channels = guide.shape
    ring = lax.axis_size(("tile", "mp"))
    low, high = neighbours(slab, UP * SIDE, 1)
    weights = conv_weights.reshape(3, 3, 3 * channels, channels)
    return pl.pallas_call(
        functools.partial(scene_kernel, rows, rows * ring),
        out_shape=jax.ShapeDtypeStruct(guide.shape, jnp.bfloat16),
        in_specs=[pl.BlockSpec(memory_space=pltpu.VMEM)] * 8,
        out_specs=pl.BlockSpec(memory_space=pltpu.VMEM),
        scratch_shapes=[
            pltpu.VMEM((rows + 2 * reach, width_px, 3 * channels), jnp.bfloat16)
            for reach in (3, 2, 1)
        ],
        compiler_params=pltpu.CompilerParams(vmem_limit_bytes=50 << 20),
        name="scene_convolutions",
    )(low, slab, high, guide_low, guide, guide_high, weights, conv_bias)


def per_device(
    tokens,
    ln_gain_one,
    ln_gain_two,
    qkv_weight,
    out_weight,
    in_weight,
    mlp_out_weight,
    proj_weight,
    land_mask,
    placement,
    guide,
    conv_weights,
    conv_bias,
):
    tiles_here, seg_rows, width = tokens.shape
    groups = lax.axis_size("tile")
    parts = lax.axis_size("mp")
    tiles_each = tiles_here // parts
    guide_low, guide_high = neighbours(guide, HALO)

    heads_local = qkv_weight.shape[2] // HEAD
    seq, qkv_all, out_all, in_all, mlp_all = gather_all(
        tokens, qkv_weight.reshape(-1, qkv_weight.shape[2]), out_weight, in_weight, mlp_out_weight
    )
    qkv_all = qkv_all.reshape(parts, 3, width, heads_local * HEAD)
    out_all = out_all.reshape(-1, width)
    in_all = in_all.reshape(-1, width)
    mlp_all = mlp_all.reshape(-1, width)

    normed = layer_norm(seq, ln_gain_one)
    projected = jnp.einsum(
        "tpd,zkde->kztpe", normed, qkv_all, preferred_element_type=jnp.float32
    ).astype(jnp.bfloat16)
    shaped = projected.reshape(3, parts, tiles_each, PATCHES, heads_local, HEAD)
    scores = jnp.einsum(
        "ztphe,ztqhe->zthpq", shaped[0], shaped[1], preferred_element_type=jnp.float32
    ) * HEAD ** (-0.5)
    soft_weights = jax.nn.softmax(scores, axis=-1).astype(jnp.bfloat16)
    context = jnp.einsum(
        "zthpq,ztqhe->tpzhe", soft_weights, shaped[2], preferred_element_type=jnp.float32
    )
    context = context.astype(jnp.bfloat16).reshape(tiles_each, PATCHES, width)
    attention = jnp.einsum("tpe,ed->tpd", context, out_all, preferred_element_type=jnp.float32)
    middle = (seq.astype(jnp.float32) + attention).astype(jnp.bfloat16)
    middle, guide_low, guide_high = lax.optimization_barrier((middle, guide_low, guide_high))
    normed_mid = layer_norm(middle, ln_gain_two)
    swap = [(i, i + 1 - 2 * (i % 2)) for i in range(groups)]

    def mlp_in(rows):
        hidden = jnp.einsum("tpd,fd->tpf", rows, in_all, preferred_element_type=jnp.float32)
        return jax.nn.gelu(hidden).astype(jnp.bfloat16)

    def mlp_out(hidden):
        return jnp.einsum("tpf,fd->tpd", hidden, mlp_all, preferred_element_type=jnp.float32)

    beside = lax.ppermute(normed_mid, "tile", swap)
    hidden, beside = lax.optimization_barrier((mlp_in(normed_mid), beside))
    beside = lax.ppermute(mlp_out(mlp_in(beside)).astype(jnp.bfloat16), "tile", swap)
    mlp_part = mlp_out(hidden) + beside.astype(jnp.float32)
    features = (middle.astype(jnp.float32) + mlp_part).astype(jnp.bfloat16)
    mask_here = lax.dynamic_slice_in_dim(
        land_mask, lax.axis_index("mp") * tiles_each, tiles_each, 0
    ).astype(jnp.bfloat16)
    embed = jnp.einsum("tpd,dc->tpc", features, proj_weight, preferred_element_type=jnp.float32)
    embed = embed.astype(jnp.bfloat16) * mask_here[:, None, None]
    channels = embed.shape[-1]

    split = embed.reshape(tiles_each, parts, seg_rows, channels).transpose(1, 0, 2, 3)
    split = lax.all_to_all(split, "mp", split_axis=0, concat_axis=0, tiled=True)
    split = split.reshape(tiles_here, seg_rows, channels)

    group_here = lax.axis_index("tile")
    slab_all = placement // tiles_here
    column_all = placement % tiles_here
    group_all = jnp.arange(placement.shape[0], dtype=jnp.int32) // tiles_here
    slab_local = lax.dynamic_slice_in_dim(slab_all, group_here * tiles_here, tiles_here, 0)
    selector = (slab_local[None, :] == jnp.arange(groups, dtype=jnp.int32)[:, None]).astype(
        jnp.bfloat16
    )
    in_slab = slab_all == group_here
    column_hot = (
        column_all[:, None] == jnp.arange(tiles_here, dtype=jnp.int32)[None, :]
    ) & in_slab[:, None]
    group_hot = group_all[:, None] == jnp.arange(groups, dtype=jnp.int32)[None, :]
    arrange = jnp.einsum(
        "tk,tg->kg", column_hot.astype(jnp.float32), group_hot.astype(jnp.float32)
    ).astype(jnp.bfloat16)
    outgoing = jnp.einsum(
        "sj,jpd->spd", selector, split, preferred_element_type=jnp.float32
    ).astype(jnp.bfloat16)
    incoming = lax.all_to_all(outgoing, "tile", split_axis=0, concat_axis=0, tiled=True)
    slab_embed = jnp.einsum(
        "kg,gpd->kpd", arrange, incoming, preferred_element_type=jnp.float32
    ).astype(jnp.bfloat16)
    return scene(slab_embed, guide, guide_low, guide_high, conv_weights, conv_bias)


def solution(mesh):
    in_specs = (
        P("tile", "mp", None),
        P(),
        P(),
        P(None, None, "mp"),
        P("mp", None),
        P("mp", None),
        P("mp", None),
        P(),
        P("tile"),
        P(),
        P(("tile", "mp"), None, None),
        P(),
        P(),
    )
    out_specs = P(("tile", "mp"), None, None)
    return jax.shard_map(
        per_device, mesh=mesh, in_specs=in_specs, out_specs=out_specs, check_vma=False
    )
```

```python
import functools

import jax
import jax.numpy as jnp
from jax import lax
from jax.experimental import pallas as pl
from jax.experimental.pallas import tpu as pltpu
from jax.sharding import PartitionSpec as P

HEAD = 64
SIDE = 16
UP = 2
PATCHES = 256
HALO = 3
SPREAD = 4
KINDS = 5


def layer_norm(values, gain):
    widened = values.astype(jnp.float32)
    centre = jnp.mean(widened, axis=-1, keepdims=True)
    spread = jnp.mean((widened - centre) ** 2, axis=-1, keepdims=True)
    return ((widened - centre) * lax.rsqrt(spread + 1e-06) * gain).astype(jnp.bfloat16)


def flip(index, bit):
    return index + bit - 2 * bit * (index // bit % 2)


def gather_kernel(
    count,
    tiles_each,
    tokens_ref,
    qkv_ref,
    out_ref,
    in_ref,
    mlp_ref,
    seq_ref,
    qkv_all,
    out_all,
    in_all,
    mlp_all,
    token_send,
    token_recv,
    own_sem,
    chain_send,
    send_sem,
    recv_sem,
):
    me_t = lax.axis_index("tile")
    me_z = lax.axis_index("mp")
    seg = tokens_ref.shape[1]
    shards = (qkv_ref, out_ref, in_ref, mlp_ref)
    gathered = (qkv_all, out_all, in_all, mlp_all)

    barrier = pltpu.get_barrier_semaphore()
    for bit in (2, 4):
        pl.semaphore_signal(
            barrier, inc=1, device_id={"tile": flip(me_t, bit), "mp": me_z},
            device_id_type=pl.DeviceIdType.MESH,
        )
    for step in range(1, count):
        pl.semaphore_signal(
            barrier, inc=1, device_id={"tile": me_t, "mp": lax.rem(me_z + step, count)},
            device_id_type=pl.DeviceIdType.MESH,
        )
    pl.semaphore_wait(barrier, 2 + count - 1)

    def piece(which, origin, owner, part=None):
        rows = gathered[which].shape[1] // SPREAD
        cols = gathered[which].shape[2]
        begin = pl.multiple_of(owner // 2 % SPREAD * rows, rows)
        if part is None:
            return (origin, pl.ds(begin, rows))
        if rows % 32 == 0:
            half = rows // 2
            return (origin, pl.ds(pl.multiple_of(begin + part * half, half), half))
        half = cols // 2
        return (origin, pl.ds(begin, rows), pl.ds(part * half, half))

    def remote(src, dst, send, recv, tile, mp):
        return pltpu.make_async_remote_copy(
            src_ref=src, dst_ref=dst, send_sem=send, recv_sem=recv,
            device_id={"tile": tile, "mp": mp}, device_id_type=pl.DeviceIdType.MESH,
        )

    token_copies = []
    for step in range(1, count):
        target = lax.rem(me_z + step, count)
        copy = remote(
            tokens_ref.at[pl.ds(target * tiles_each, tiles_each)],
            seq_ref.at[:, pl.ds(pl.multiple_of(me_z * seg, seg), seg)],
            token_send.at[step], token_recv.at[step], me_t, target,
        )
        copy.start()
        token_copies.append(copy)
    own_tokens = pltpu.make_async_copy(
        tokens_ref.at[pl.ds(me_z * tiles_each, tiles_each)],
        seq_ref.at[:, pl.ds(pl.multiple_of(me_z * seg, seg), seg)],
        token_send.at[0],
    )
    own_tokens.start()

    def own_part(which):
        if which == 0:
            return shards[which]
        rows = shards[which].shape[0] // 2
        return shards[which].at[pl.ds(pl.multiple_of(me_t % 2 * rows, rows), rows)]

    def own_piece(which):
        rows = gathered[which].shape[1] // SPREAD
        base = 0 if which == 0 else me_t % 2 * SPREAD
        place = base + me_t // 2 % SPREAD
        return shards[which].at[pl.ds(pl.multiple_of(place * rows, rows), rows)]

    def along(which, step):
        return remote(
            own_piece(which), gathered[which].at[piece(which, me_z, me_t)],
            chain_send.at[which, step], recv_sem.at[which, me_z, 0],
            me_t, lax.rem(me_z + step, count),
        )

    def first_sends(which):
        for step in range(1, count):
            along(which, step).start()

    def source(index):
        below, above = me_z, count - 1 - me_z
        least = jnp.minimum(below, above)
        paired = index < 2 * least
        down_side = jnp.where(paired, index % 2 == 0, below > above)
        far = jnp.where(paired, index // 2 + 1, index - least + 1)
        return jnp.where(down_side, me_z - far, me_z + far)

    def ring(which, origin, owner, kind, part, bit):
        where = piece(which, origin, owner, part)
        ref = gathered[which].at[where]
        return remote(
            ref, ref, send_sem.at[which, origin, kind], recv_sem.at[which, origin, kind],
            flip(me_t, bit), me_z,
        )

    first_bit = 2 + 2 * (me_t % 2)
    second_bit = 4 - 2 * (me_t % 2)
    outward = {
        1: (me_t, None, first_bit),
        2: (me_t, None, second_bit),
        3: (flip(me_t, first_bit), 0, second_bit),
        4: (flip(me_t, second_bit), 1, first_bit),
    }

    def go(which, origin, kind):
        owner, part, bit = outward[kind]
        ring(which, origin, owner, kind, part, bit).start()

    def arrived(which, origin, kind):
        owner, part, bit = outward[kind]
        ring(which, origin, flip(owner, bit), kind, part, bit).wait_recv()

    def stage_a(which, index):
        origin = source(index)
        where = gathered[which].at[piece(which, origin, me_t)]
        remote(
            where, where, chain_send.at[which, 0], recv_sem.at[which, origin, 0], me_t, origin
        ).wait_recv()
        go(which, origin, 1)
        go(which, origin, 2)

    def stage_b(which, index):
        origin = source(index)
        arrived(which, origin, 1)
        go(which, origin, 3)
        arrived(which, origin, 2)
        go(which, origin, 4)

    def stage_c(which, index):
        origin = source(index)
        arrived(which, origin, 3)
        arrived(which, origin, 4)

    own_copies = [
        pltpu.make_async_copy(own_part(which), gathered[which].at[me_z], own_sem.at[which])
        for which in range(4)
    ]
    first_sends(0)
    for copy in own_copies:
        copy.start()
    first_sends(1)

    units = [(which, index) for which in range(4) for index in range(count - 1)]
    stages = (stage_a, stage_b, stage_c)
    for tick in range(len(units) + 2):
        for late, stage in enumerate(stages):
            at = tick - late
            if 0 <= at < len(units):
                stage(*units[at])
                if late == 0 and units[at][1] == 0 and units[at][0] + 2 < 4:
                    first_sends(units[at][0] + 2)

    own_tokens.wait()
    for copy in token_copies:
        copy.wait()
    for copy in own_copies:
        copy.wait()
    for which in range(4):
        for step in range(1, count):
            along(which, step).wait_send()
        for index in range(count - 1):
            origin = source(index)
            for kind in range(1, KINDS):
                owner, part, bit = outward[kind]
                ring(which, origin, owner, kind, part, bit).wait_send()


def gather_all(tokens, qkv, out, into, mlp):
    count = lax.axis_size("mp")
    tiles_each = tokens.shape[0] // count
    any_space = pl.BlockSpec(memory_space=pl.ANY)
    return pl.pallas_call(
        functools.partial(gather_kernel, count, tiles_each),
        out_shape=(
            jax.ShapeDtypeStruct((tiles_each, PATCHES, tokens.shape[2]), jnp.bfloat16),
        ) + tuple(
            jax.ShapeDtypeStruct((count, part.shape[0] // cut, part.shape[1]), jnp.bfloat16)
            for part, cut in ((qkv, 1), (out, 2), (into, 2), (mlp, 2))
        ),
        in_specs=[any_space] * 5,
        out_specs=(any_space,) * 5,
        scratch_shapes=[
            pltpu.SemaphoreType.DMA((count,)),
            pltpu.SemaphoreType.DMA((count,)),
            pltpu.SemaphoreType.DMA((4,)),
            pltpu.SemaphoreType.DMA((4, count)),
            pltpu.SemaphoreType.DMA((4, count, KINDS)),
            pltpu.SemaphoreType.DMA((4, count, KINDS)),
        ],
        compiler_params=pltpu.CompilerParams(collective_id=0, has_side_effects=True),
        name="gather_weights",
    )(tokens, qkv, out, into, mlp)


def neighbours(block, width, dim=0):
    axes = ("tile", "mp")
    count = lax.axis_size(axes)
    forward = [(i, i + 1) for i in range(count - 1)]
    backward = [(target, source) for source, target in forward]
    low = lax.ppermute(lax.slice_in_dim(block, block.shape[dim] - width, None, axis=dim), axes, forward)
    high = lax.ppermute(lax.slice_in_dim(block, 0, width, axis=dim), axes, backward)
    return low, high


def scene_kernel(
    row_count,
    scene_rows,
    low_ref,
    mid_ref,
    high_ref,
    guide_low,
    guide_mid,
    guide_high,
    weights_ref,
    bias_ref,
    result_ref,
    guided_buf,
    first_buf,
    second_buf,
):
    here = lax.axis_index(("tile", "mp"))
    width_px, channels = guide_mid.shape[1:]
    cols = width_px // UP
    column = lax.broadcasted_iota(jnp.int32, (width_px, channels), 0)
    spread = (
        lax.broadcasted_iota(jnp.int32, (width_px, cols), 0) // UP
        == lax.broadcasted_iota(jnp.int32, (width_px, cols), 1)
    ).astype(jnp.bfloat16)

    def put(buffer, row, values):
        before = jnp.where(column == 0, 0.0, pltpu.roll(values, 1, 0))
        after = jnp.where(column == width_px - 1, 0.0, pltpu.roll(values, width_px - 1, 0))
        buffer[row, :, pl.ds(0, channels)] = before.astype(jnp.bfloat16)
        buffer[row, :, pl.ds(channels, channels)] = values.astype(jnp.bfloat16)
        buffer[row, :, pl.ds(2 * channels, channels)] = after.astype(jnp.bfloat16)

    def token_row(row):
        inner = mid_ref.shape[1] // SIDE
        if row < UP:
            ref, at = low_ref, row
        elif row < UP + inner:
            ref, at = mid_ref, row - UP
        else:
            ref, at = high_ref, row - UP - inner
        line = ref[:, pl.ds(at * SIDE, SIDE), :].reshape(cols, channels)
        return jnp.dot(spread, line, preferred_element_type=jnp.float32)

    def guide_row(row):
        if row < HALO:
            return guide_low[row]
        if row < HALO + row_count:
            return guide_mid[row - HALO]
        return guide_high[row - HALO - row_count]

    for row in range(row_count + 2 * HALO):
        put(guided_buf, row, token_row((row + 1) // UP) + guide_row(row).astype(jnp.float32))

    def conv(buffer, layer, row):
        total = jnp.zeros((2 * width_px, channels), jnp.float32) + bias_ref[pl.ds(layer, 1), :]
        for shift in range(3):
            window = buffer[pl.ds(row + shift, 2)].reshape(2 * width_px, 3 * channels)
            total += jnp.dot(window, weights_ref[layer, shift], preferred_element_type=jnp.float32)
        return total

    for layer, source, target in ((0, guided_buf, first_buf), (1, first_buf, second_buf)):
        reach = HALO - 1 - layer

        @pl.loop(0, row_count // 2 + reach)
        def _(pair):
            values = jax.nn.gelu(conv(source, layer, 2 * pair))
            for part in range(2):
                at = here * row_count - reach + 2 * pair + part
                keep = (at >= 0) & (at < scene_rows)
                line = values[part * width_px : (part + 1) * width_px]
                put(target, 2 * pair + part, jnp.where(keep, line, 0.0))

    @pl.loop(0, row_count // 2)
    def _(pair):
        values = conv(second_buf, 2, 2 * pair).reshape(2, width_px, channels)
        base = guided_buf[pl.ds(2 * pair + HALO, 2), :, pl.ds(channels, channels)]
        result_ref[pl.ds(2 * pair, 2)] = (base.astype(jnp.float32) + values).astype(jnp.bfloat16)


def scene(slab, guide, guide_low, guide_high, conv_weights, conv_bias):
    rows, width_px, channels = guide.shape
    ring = lax.axis_size(("tile", "mp"))
    low, high = neighbours(slab, UP * SIDE, 1)
    weights = conv_weights.reshape(3, 3, 3 * channels, channels)
    return pl.pallas_call(
        functools.partial(scene_kernel, rows, rows * ring),
        out_shape=jax.ShapeDtypeStruct(guide.shape, jnp.bfloat16),
        in_specs=[pl.BlockSpec(memory_space=pltpu.VMEM)] * 8,
        out_specs=pl.BlockSpec(memory_space=pltpu.VMEM),
        scratch_shapes=[
            pltpu.VMEM((rows + 2 * reach, width_px, 3 * channels), jnp.bfloat16)
            for reach in (3, 2, 1)
        ],
        compiler_params=pltpu.CompilerParams(vmem_limit_bytes=50 << 20),
        name="scene_convolutions",
    )(low, slab, high, guide_low, guide, guide_high, weights, conv_bias)


def per_device(
    tokens,
    ln_gain_one,
    ln_gain_two,
    qkv_weight,
    out_weight,
    in_weight,
    mlp_out_weight,
    proj_weight,
    land_mask,
    placement,
    guide,
    conv_weights,
    conv_bias,
):
    tiles_here, seg_rows, width = tokens.shape
    groups = lax.axis_size("tile")
    parts = lax.axis_size("mp")
    tiles_each = tiles_here // parts
    guide_low, guide_high = neighbours(guide, HALO)

    swap = [(i, i + 1 - 2 * (i % 2)) for i in range(groups)]
    heads_local = qkv_weight.shape[2] // HEAD // 2
    half = lax.dynamic_slice_in_dim(
        qkv_weight, lax.axis_index("tile") % 2 * (heads_local * HEAD), heads_local * HEAD, 2
    )
    seq, qkv_all, out_all, in_all, mlp_all = gather_all(
        tokens, half.reshape(-1, half.shape[2]), out_weight, in_weight, mlp_out_weight
    )
    qkv_all = qkv_all.reshape(parts, 3, width, heads_local * HEAD)
    out_all = out_all.reshape(-1, width)
    in_all = in_all.reshape(-1, width)
    mlp_all = mlp_all.reshape(-1, width)

    def project(rows):
        return jnp.einsum(
            "tpd,zkde->kztpe", rows, qkv_all, preferred_element_type=jnp.float32
        ).astype(jnp.bfloat16)

    def attend(projected):
        shaped = projected.reshape(3, parts, tiles_each, PATCHES, heads_local, HEAD)
        scores = jnp.einsum(
            "ztphe,ztqhe->zthpq", shaped[0], shaped[1], preferred_element_type=jnp.float32
        ) * HEAD ** (-0.5)
        soft_weights = jax.nn.softmax(scores, axis=-1).astype(jnp.bfloat16)
        context = jnp.einsum(
            "zthpq,ztqhe->tpzhe", soft_weights, shaped[2], preferred_element_type=jnp.float32
        )
        context = context.astype(jnp.bfloat16).reshape(tiles_each, PATCHES, out_all.shape[0])
        return jnp.einsum("tpe,ed->tpd", context, out_all, preferred_element_type=jnp.float32)

    normed = layer_norm(seq, ln_gain_one)
    beside = lax.ppermute(normed, "tile", swap)
    projected, beside = lax.optimization_barrier((project(normed), beside))
    beside = lax.ppermute(attend(project(beside)).astype(jnp.bfloat16), "tile", swap)
    attention = attend(projected) + beside.astype(jnp.float32)
    middle = (seq.astype(jnp.float32) + attention).astype(jnp.bfloat16)
    middle, guide_low, guide_high = lax.optimization_barrier((middle, guide_low, guide_high))
    normed_mid = layer_norm(middle, ln_gain_two)

    def mlp_in(rows):
        hidden = jnp.einsum("tpd,fd->tpf", rows, in_all, preferred_element_type=jnp.float32)
        return jax.nn.gelu(hidden).astype(jnp.bfloat16)

    def mlp_out(hidden):
        return jnp.einsum("tpf,fd->tpd", hidden, mlp_all, preferred_element_type=jnp.float32)

    beside = lax.ppermute(normed_mid, "tile", swap)
    hidden, beside = lax.optimization_barrier((mlp_in(normed_mid), beside))
    beside = lax.ppermute(mlp_out(mlp_in(beside)).astype(jnp.bfloat16), "tile", swap)
    mlp_part = mlp_out(hidden) + beside.astype(jnp.float32)
    features = (middle.astype(jnp.float32) + mlp_part).astype(jnp.bfloat16)
    mask_here = lax.dynamic_slice_in_dim(
        land_mask, lax.axis_index("mp") * tiles_each, tiles_each, 0
    ).astype(jnp.bfloat16)
    embed = jnp.einsum("tpd,dc->tpc", features, proj_weight, preferred_element_type=jnp.float32)
    embed = embed.astype(jnp.bfloat16) * mask_here[:, None, None]
    channels = embed.shape[-1]

    split = embed.reshape(tiles_each, parts, seg_rows, channels).transpose(1, 0, 2, 3)
    split = lax.all_to_all(split, "mp", split_axis=0, concat_axis=0, tiled=True)
    split = split.reshape(tiles_here, seg_rows, channels)

    group_here = lax.axis_index("tile")
    slab_all = placement // tiles_here
    column_all = placement % tiles_here
    group_all = jnp.arange(placement.shape[0], dtype=jnp.int32) // tiles_here
    slab_local = lax.dynamic_slice_in_dim(slab_all, group_here * tiles_here, tiles_here, 0)
    selector = (slab_local[None, :] == jnp.arange(groups, dtype=jnp.int32)[:, None]).astype(
        jnp.bfloat16
    )
    in_slab = slab_all == group_here
    column_hot = (
        column_all[:, None] == jnp.arange(tiles_here, dtype=jnp.int32)[None, :]
    ) & in_slab[:, None]
    group_hot = group_all[:, None] == jnp.arange(groups, dtype=jnp.int32)[None, :]
    arrange = jnp.einsum(
        "tk,tg->kg", column_hot.astype(jnp.float32), group_hot.astype(jnp.float32)
    ).astype(jnp.bfloat16)
    outgoing = jnp.einsum(
        "sj,jpd->spd", selector, split, preferred_element_type=jnp.float32
    ).astype(jnp.bfloat16)
    incoming = lax.all_to_all(outgoing, "tile", split_axis=0, concat_axis=0, tiled=True)
    slab_embed = jnp.einsum(
        "kg,gpd->kpd", arrange, incoming, preferred_element_type=jnp.float32
    ).astype(jnp.bfloat16)
    return scene(slab_embed, guide, guide_low, guide_high, conv_weights, conv_bias)


def solution(mesh):
    in_specs = (
        P("tile", "mp", None),
        P(),
        P(),
        P(None, None, "mp"),
        P("mp", None),
        P("mp", None),
        P("mp", None),
        P(),
        P("tile"),
        P(),
        P(("tile", "mp"), None, None),
        P(),
        P(),
    )
    out_specs = P(("tile", "mp"), None, None)
    return jax.shard_map(
        per_device, mesh=mesh, in_specs=in_specs, out_specs=out_specs, check_vma=False
    )
```
